512 devices in a mesh: pairs: 512 (over z, x, y, core).
Axes of the slice: x: 4, y: 4, z: 16, core: 2. Of those that a mesh axis runs over, the one named last changes fastest.
Arguments:
- coeffs: bfloat16 [32768, 128, 128], P('pairs'), may hold values from -6 to 6
- target_box: int32 [3, 32768], P(None, 'pairs'), may hold values from 0 to 4095
- source_box: int32 [3, 32768], P(None, 'pairs'), may hold values from 0 to 4095
- interp: bfloat16 [3, 2, 2, 128, 128], replicated, may hold values from -0.375 to 0.375
Outputs:
- result: bfloat16 [32768, 128, 128], P('pairs')
The draws below stay inside these ranges and needn't reach their ends.
All inputs are finite; a program needn't handle non-finite values.
Results may differ from the reference program's by a relative error of at most 0.02.
Values may be sent and summed in bfloat16 or wider, within the bound.
A program may use at most 64 MiB of HBM per device.

```python
import math
import jax
import jax.numpy as jnp
from jax import lax

CW = 128
LEVELS = 3
PAIR_DEV = 64
NV = 128
NP = 32768
N_PAIRS = 512


def place_ends(values, stream_key, least, high):
    longest = values.shape.index(max(values.shape))
    spots = []
    for shift in (0, 1):
        where = [jax.random.randint(jax.random.fold_in(stream_key, axis), (), 0, length) for axis, length in enumerate(values.shape)]
        where[longest] = (where[longest] + shift) % values.shape[longest]
        spots.append(tuple(where))
    return values.at[spots[0]].set(least).at[spots[1]].set(high)


def levels(rng, shape, cuts, smallest, high):
    gain = 1.0
    for position, parts in cuts:
        heights = jax.random.uniform(jax.random.fold_in(jax.random.fold_in(rng, 6), position), (parts,), jnp.float32, smallest / len(cuts), high / len(cuts))
        gain = gain * jnp.repeat(jnp.exp(heights), shape[position] // parts).reshape((-1,) + (1,) * (len(shape) - 1 - position))
    return gain


def normal_values(rng, dims, deviation, most, pieces=(), kind=jnp.bfloat16):
    drawn = deviation * jax.random.normal(rng, dims, jnp.float32)
    if pieces:
        drawn = drawn * levels(rng, dims, pieces, -0.22, 0.18)
    return jnp.clip(drawn, -most, most).astype(kind)


def setup_inputs(seed: int = 0) -> dict:
    key_of = jax.random.split(jax.random.key(seed), 5)
    coeffs = normal_values(key_of[0], (NP, NV, CW), 1.0, 6.0, ((0, 512),))
    target_box = place_ends(jax.random.randint(key_of[1], (LEVELS, NP), 0, 4096), jax.random.fold_in(key_of[1], 1), 0, 4095).astype(jnp.int32)
    source_box = place_ends(jax.random.randint(key_of[2], (LEVELS, NP), 0, 4096), jax.random.fold_in(key_of[2], 1), 0, 4095).astype(jnp.int32)
    interp = normal_values(key_of[3], (LEVELS, 2, 2, CW, CW), (2 * CW) ** -0.5, 0.375)
    return {"coeffs": coeffs, "target_box": target_box, "source_box": source_box, "interp": interp}


def rotate(current, target_box, source_box, rung_index):
    offsets = jnp.mod(target_box[rung_index] - source_box[rung_index], 4096).astype(jnp.float32)
    angles = offsets * (2.0 * math.pi / 4096.0)
    cosine = jnp.cos(angles)[:, None, None]
    sines = jnp.sin(angles)[:, None, None]
    widened = current.astype(jnp.float32)
    rank_count = widened.shape[-1] // 2
    real_part = widened[..., :rank_count]
    imag_part = widened[..., rank_count:]
    turned = jnp.concatenate([cosine * real_part - sines * imag_part, sines * real_part + cosine * imag_part], axis=-1)
    return turned.astype(jnp.bfloat16)


def reference(coeffs, target_box, source_box, interp):
    total_rows, vectors, columns = coeffs.shape
    log_count = N_PAIRS.bit_length() - 1
    block = math.gcd(vectors, 16)
    blocks = coeffs.reshape(total_rows, vectors // block, block, columns).transpose(1, 0, 2, 3)
    half_rows = PAIR_DEV // 2

    def run(current):
        for rung_index in range(LEVELS):
            bit_place = log_count - 1 - rung_index
            span = 2 ** bit_place
            groups = N_PAIRS // (2 * span)
            rotated = rotate(current, target_box, source_box, rung_index).astype(jnp.float32)
            shaped = rotated.reshape(groups, 2, span, 2, half_rows, block, columns)
            weights32 = interp[rung_index].astype(jnp.float32)
            results = []
            for side_bit in range(2):
                first = shaped[:, 0, :, side_bit]
                second = shaped[:, 1, :, side_bit]
                combined = jnp.einsum("asknd,tde->asktne", first, weights32[:, 0], precision=lax.Precision.HIGHEST)
                combined = combined + jnp.einsum("asknd,tde->asktne", second, weights32[:, 1], precision=lax.Precision.HIGHEST)
                results.append(combined)
            stacked = jnp.stack(results, axis=1)
            current = stacked.reshape(total_rows, block, columns).astype(jnp.bfloat16)
        return current

    mapped = lax.map(run, blocks)
    return mapped.transpose(1, 0, 2, 3).reshape(total_rows, vectors, columns)
```

```python
import functools
import math

import jax
import jax.numpy as jnp
from jax import lax
from jax.experimental import pallas as pl
from jax.experimental.pallas import tpu as pltpu
from jax.sharding import PartitionSpec as P

MESH = pl.DeviceIdType.MESH
GROUP = 8
FAR = (4, 3, -3, 2, -2, 1, -1)


def kernel(n, coeffs, tbox, sbox, interp, out, got, tab, tabs, phase, wcat,
           send, recv, tsend, trecv, own):
    stride = n // GROUP
    me = lax.axis_index("pairs")
    e_me = me // stride
    rest = me % stride

    def peer(d):
        return ((e_me + d + GROUP) % GROUP) * stride + rest

    def slot_copy(d, g):
        to = (e_me + d + GROUP) % GROUP
        return pltpu.make_async_remote_copy(
            src_ref=coeffs.at[to * GROUP + g],
            dst_ref=got.at[d % GROUP, g],
            send_sem=send.at[d % GROUP, g],
            recv_sem=recv.at[d % GROUP, g],
            device_id=(peer(d),),
            device_id_type=MESH,
        )

    def table_copy(d):
        return pltpu.make_async_remote_copy(
            src_ref=tab,
            dst_ref=tabs.at[d % GROUP],
            send_sem=tsend.at[d % GROUP],
            recv_sem=trecv.at[d % GROUP],
            device_id=(peer(d),),
            device_id_type=MESH,
        )

    barrier = pltpu.get_barrier_semaphore()
    for d in FAR:
        pl.semaphore_signal(barrier, inc=1, device_id=(peer(d),), device_id_type=MESH)
    own_copy = pltpu.make_async_copy(
        coeffs.at[pl.ds(e_me * GROUP, GROUP)], got.at[0], own.at[0]
    )
    own_copy.start()
    turn = ((tbox[...] - sbox[...]) & 4095).astype(jnp.float32) * (2.0 * math.pi / 4096.0)
    tab[0:3, :] = jnp.concatenate([jnp.cos(turn), jnp.sin(turn)], axis=1)
    tab[3:8, :] = jnp.zeros((5, 128), jnp.float32)
    pl.semaphore_wait(barrier, len(FAR))

    for d in FAR:
        table_copy(d).start()

    def start_slots(g, carry):
        for d in FAR:
            slot_copy(d, g).start()
        return carry

    lax.fori_loop(0, GROUP, start_slots, 0)

    for l in range(3):
        for t in range(2):
            for c in range(2):
                wcat[l, c * 128:(c + 1) * 128, t * 128:(t + 1) * 128] = interp[l, t, c]

    tabs[0] = tab[...]
    for d in FAR:
        table_copy(d).wait_recv()
    to_scalar = pltpu.make_async_copy(tabs, phase, own.at[1])
    to_scalar.start()
    to_scalar.wait()
    own_copy.wait()

    sign = jnp.where(lax.broadcasted_iota(jnp.int32, (1, 128), 1) < 64, -1.0, 1.0)
    f0, f1, f2 = e_me // 4, e_me // 2 % 2, e_me % 2

    def turned(x, e, l, slot):
        at = (e_me - e + GROUP) % GROUP
        c = phase[at, l, slot]
        s = phase[at, l, 64 + slot]
        return (c * x + (s * sign) * pltpu.roll(x, 64, 1)).astype(jnp.bfloat16)

    def level(l, pieces):
        rows = jnp.concatenate([jnp.concatenate(p, axis=1) for p in pieces], axis=0)
        return jnp.dot(rows, wcat[l], preferred_element_type=jnp.float32)

    def work(g, carry):
        for d in FAR:
            slot_copy(d, g).wait_recv()
        y = level(0, [
            [turned(got[(e_me - e + GROUP) % GROUP, g].astype(jnp.float32), e, 0,
                    e_me * 8 + g)
             for e in (e1 * 2 + e2, 4 + e1 * 2 + e2)]
            for e1 in range(2) for e2 in range(2)
        ])
        y = level(1, [
            [turned(y[(e1 * 2 + e2) * 128:(e1 * 2 + e2 + 1) * 128, t0 * 128:(t0 + 1) * 128],
                    f0 * 4 + e1 * 2 + e2, 1, f1 * 32 + f2 * 16 + g * 2 + t0)
             for e1 in range(2)]
            for e2 in range(2) for t0 in range(2)
        ])
        y = level(2, [
            [turned(y[(e2 * 2 + t0) * 128:(e2 * 2 + t0 + 1) * 128, t1 * 128:(t1 + 1) * 128],
                    f0 * 4 + f1 * 2 + e2, 2, f2 * 32 + g * 4 + t0 * 2 + t1)
             for e2 in range(2)]
            for t0 in range(2) for t1 in range(2)
        ])
        for t01 in range(4):
            for t2 in range(2):
                out[g * 8 + t01 * 2 + t2] = y[
                    t01 * 128:(t01 + 1) * 128, t2 * 128:(t2 + 1) * 128
                ].astype(jnp.bfloat16)
        return carry

    lax.fori_loop(0, GROUP, work, 0)

    def finish(g, carry):
        for d in FAR:
            slot_copy(d, g).wait_send()
        return carry

    for d in FAR:
        table_copy(d).wait_send()
    lax.fori_loop(0, GROUP, finish, 0)


def solution(mesh):
    n = mesh.shape["pairs"]

    def body(coeffs, target_box, source_box, interp):
        _, rows, columns = coeffs.shape
        dma = pltpu.SemaphoreType.DMA
        return pl.pallas_call(
            functools.partial(kernel, n),
            out_shape=jax.ShapeDtypeStruct(coeffs.shape, jnp.bfloat16),
            in_specs=[pl.BlockSpec(memory_space=pltpu.HBM)]
            + [pl.BlockSpec(memory_space=pltpu.VMEM)] * 3,
            out_specs=pl.BlockSpec(memory_space=pltpu.VMEM),
            scratch_shapes=[
                pltpu.VMEM((GROUP, GROUP, rows, columns), jnp.bfloat16),
                pltpu.VMEM((8, 128), jnp.float32),
                pltpu.VMEM((GROUP, 8, 128), jnp.float32),
                pltpu.SMEM((GROUP, 8, 128), jnp.float32),
                pltpu.VMEM((3, 256, 256), jnp.bfloat16),
                dma((GROUP, GROUP)),
                dma((GROUP, GROUP)),
                dma((GROUP,)),
                dma((GROUP,)),
                dma((2,)),
            ],
            compiler_params=pltpu.CompilerParams(
                collective_id=0, has_side_effects=True, vmem_limit_bytes=32 << 20
            ),
            name="butterfly",
        )(coeffs, target_box, source_box, interp)

    placed = (P("pairs", None, None), P(None, "pairs"), P(None, "pairs"), P())
    return jax.shard_map(
        body, mesh=mesh, in_specs=placed, out_specs=P("pairs", None, None), check_vma=False
    )
```

```python
import functools
import math

import jax
import jax.numpy as jnp
from jax import lax
from jax.experimental import pallas as pl
from jax.experimental.pallas import tpu as pltpu
from jax.sharding import PartitionSpec as P

MESH = pl.DeviceIdType.MESH
GROUP = 8
ALL = (1, -1, 2, -2, 3, -3, 4)


def kernel(n, coeffs, tbox_hbm, sbox_hbm, interp_hbm, out, tbox, sbox, interp, got, tab,
           tabs, waves, phase, wcat, send, recv, tsend, trecv, known, local):
    stride = n // GROUP
    me = lax.axis_index("pairs")
    e_me = me // stride
    rest = me % stride

    def block(d):
        return (e_me + d + GROUP) % GROUP

    def remote(src, dst, ssem, rsem, d):
        return pltpu.make_async_remote_copy(
            src_ref=src, dst_ref=dst, send_sem=ssem, recv_sem=rsem,
            device_id=(block(d) * stride + rest,), device_id_type=MESH,
        )

    def slot_copy(d, g):
        return remote(coeffs.at[block(d) * GROUP + g], got.at[d % GROUP, g],
                      send.at[d % GROUP, g], recv.at[d % GROUP, g], d)

    def table_copy(d):
        return remote(tab, tabs.at[d % GROUP], tsend.at[d % GROUP], trecv.at[d % GROUP], d)

    def tell(sem, d):
        pl.semaphore_signal(known.at[sem], inc=1, device_id=(block(d) * stride + rest,),
                            device_id_type=MESH)

    def for_slots(first, last, moves):
        def step(g, carry):
            for d in moves:
                slot_copy(d, g).start()
            return carry
        lax.fori_loop(first, last, step, 0)

    barrier = pltpu.get_barrier_semaphore()
    for d in (1, -1):
        pl.semaphore_signal(barrier, inc=1, device_id=(block(d) * stride + rest,),
                            device_id_type=MESH)
    boxes = [
        pltpu.make_async_copy(tbox_hbm, tbox, local.at[0]),
        pltpu.make_async_copy(sbox_hbm, sbox, local.at[1]),
    ]
    own_copy = pltpu.make_async_copy(
        coeffs.at[pl.ds(e_me * GROUP, GROUP)], got.at[0], local.at[2]
    )
    weights_copy = pltpu.make_async_copy(interp_hbm, interp, local.at[3])
    for copy in boxes:
        copy.start()
    own_copy.start()
    weights_copy.start()
    for copy in boxes:
        copy.wait()
    turn = (tbox[...] - sbox[...]) & 4095
    tab[0:1, :] = jnp.concatenate([turn[0:1], turn[1:2]], axis=1)
    tab[1:2, :] = jnp.concatenate([turn[2:3], turn[2:3]], axis=1)
    tabs[0] = tab[...]

    pl.semaphore_wait(barrier, 2)
    tell(0, 1)
    tell(1, -1)
    for d in (1, -1):
        table_copy(d).start()
    for_slots(4, 8, (1, -1))
    pl.semaphore_wait(known.at[0], 1)
    pl.semaphore_wait(known.at[1], 1)
    tell(2, 1)
    tell(3, -1)
    for d in (2, -2):
        table_copy(d).start()
    for_slots(6, 8, (2, -2))
    pl.semaphore_wait(known.at[2], 1)
    pl.semaphore_wait(known.at[3], 1)
    tell(4, 1)
    for d in (3, -3):
        table_copy(d).start()
    pl.semaphore_wait(known.at[4], 1)
    table_copy(4).start()
    for_slots(0, 4, (4, 3, -3, 2, -2, 1, -1))
    for_slots(4, 6, (4, 3, -3, 2, -2))
    for_slots(6, 8, (4, 3, -3))

    weights_copy.wait()
    for l in range(3):
        for t in range(2):
            for c in range(2):
                wcat[l, c * 128:(c + 1) * 128, t * 128:(t + 1) * 128] = interp[l, t, c]

    for d in ALL:
        table_copy(d).wait_recv()
    angle = tabs[...].astype(jnp.float32) * (2.0 * math.pi / 4096.0)
    waves[0] = jnp.cos(angle)
    waves[1] = jnp.sin(angle)
    to_scalar = pltpu.make_async_copy(waves, phase, local.at[4])
    to_scalar.start()
    to_scalar.wait()
    own_copy.wait()

    sign = jnp.where(lax.broadcasted_iota(jnp.int32, (1, 128), 1) < 64, -1.0, 1.0)
    f0, f1, f2 = e_me // 4, e_me // 2 % 2, e_me % 2

    def turned(x, e, l, slot):
        at = (e_me - e + GROUP) % GROUP
        c = phase[0, at, l // 2, l % 2 * 64 + slot]
        s = phase[1, at, l // 2, l % 2 * 64 + slot]
        return (c * x + (s * sign) * pltpu.roll(x, 64, 1)).astype(jnp.bfloat16)

    def level(l, pieces):
        rows = jnp.concatenate([jnp.concatenate(p, axis=1) for p in pieces], axis=0)
        return jnp.dot(rows, wcat[l], preferred_element_type=jnp.float32)

    def work(g, carry):
        for d in ALL:
            slot_copy(d, g).wait_recv()
        y = level(0, [
            [turned(got[(e_me - e + GROUP) % GROUP, g].astype(jnp.float32), e, 0,
                    e_me * 8 + g)
             for e in (e1 * 2 + e2, 4 + e1 * 2 + e2)]
            for e1 in range(2) for e2 in range(2)
        ])
        y = level(1, [
            [turned(y[(e1 * 2 + e2) * 128:(e1 * 2 + e2 + 1) * 128, t0 * 128:(t0 + 1) * 128],
                    f0 * 4 + e1 * 2 + e2, 1, f1 * 32 + f2 * 16 + g * 2 + t0)
             for e1 in range(2)]
            for e2 in range(2) for t0 in range(2)
        ])
        y = level(2, [
            [turned(y[(e2 * 2 + t0) * 128:(e2 * 2 + t0 + 1) * 128, t1 * 128:(t1 + 1) * 128],
                    f0 * 4 + f1 * 2 + e2, 2, f2 * 32 + g * 4 + t0 * 2 + t1)
             for e2 in range(2)]
            for t0 in range(2) for t1 in range(2)
        ])
        for t01 in range(4):
            for t2 in range(2):
                out[g * 8 + t01 * 2 + t2] = y[
                    t01 * 128:(t01 + 1) * 128, t2 * 128:(t2 + 1) * 128
                ].astype(jnp.bfloat16)
        return carry

    lax.fori_loop(0, GROUP, work, 0)

    for d in ALL:
        table_copy(d).wait_send()

    def finish(g, carry):
        for d in ALL:
            slot_copy(d, g).wait_send()
        return carry

    lax.fori_loop(0, GROUP, finish, 0)


def solution(mesh):
    n = mesh.shape["pairs"]

    def body(coeffs, target_box, source_box, interp):
        _, rows, columns = coeffs.shape
        dma = pltpu.SemaphoreType.DMA
        return pl.pallas_call(
            functools.partial(kernel, n),
            out_shape=pltpu.VMEM(coeffs.shape, jnp.bfloat16),
            in_specs=[pl.BlockSpec(memory_space=pltpu.HBM)] * 4,
            out_specs=pl.BlockSpec(memory_space=pltpu.VMEM),
            scratch_shapes=[
                pltpu.VMEM(target_box.shape, jnp.int32),
                pltpu.VMEM(source_box.shape, jnp.int32),
                pltpu.VMEM(interp.shape, jnp.bfloat16),
                pltpu.VMEM((GROUP, GROUP, rows, columns), jnp.bfloat16),
                pltpu.VMEM((2, 128), jnp.int32),
                pltpu.VMEM((GROUP, 2, 128), jnp.int32),
                pltpu.VMEM((2, GROUP, 2, 128), jnp.float32),
                pltpu.SMEM((2, GROUP, 2, 128), jnp.float32),
                pltpu.VMEM((3, 256, 256), jnp.bfloat16),
                dma((GROUP, GROUP)),
                dma((GROUP, GROUP)),
                dma((GROUP,)),
                dma((GROUP,)),
                pltpu.SemaphoreType.REGULAR((5,)),
                dma((5,)),
            ],
            compiler_params=pltpu.CompilerParams(
                collective_id=0, has_side_effects=True, vmem_limit_bytes=32 << 20
            ),
            name="butterfly",
        )(*(
            pltpu.with_memory_space_constraint(a, pltpu.HBM)
            for a in (coeffs, target_box, source_box, interp)
        ))

    placed = (P("pairs", None, None), P(None, "pairs"), P(None, "pairs"), P())
    return jax.shard_map(
        body, mesh=mesh, in_specs=placed, out_specs=P("pairs", None, None), check_vma=False
    )
```

```python
import functools
import math

import jax
import jax.numpy as jnp
from jax import lax
from jax.experimental import pallas as pl
from jax.experimental.pallas import tpu as pltpu
from jax.sharding import PartitionSpec as P

MESH = pl.DeviceIdType.MESH
GROUP = 8
LATER = ((2, 6, 8, 10, 24, 22, 20, 20), (2, 5, 8, 10, 24, 28, 28, 20))
ALL = (1, -1, 2, -2, 3, -3, 4)


def kernel(n, coeffs, tbox_hbm, sbox_hbm, interp_hbm, out, tbox, sbox, interp, got, tab,
           tabs, waves, phase, wcat, send, recv, tsend, trecv, known, local):
    stride = n // GROUP
    me = lax.axis_index("pairs")
    e_me = me // stride
    rest = me % stride

    def block(d):
        return (e_me + d + GROUP) % GROUP

    def remote(src, dst, ssem, rsem, d):
        return pltpu.make_async_remote_copy(
            src_ref=src, dst_ref=dst, send_sem=ssem, recv_sem=rsem,
            device_id=(block(d) * stride + rest,), device_id_type=MESH,
        )

    def slot_copy(d, g):
        return remote(coeffs.at[block(d) * GROUP + g], got.at[d % GROUP, g],
                      send.at[d % GROUP, g], recv.at[d % GROUP, g], d)

    def table_copy(d):
        return remote(tab, tabs.at[d % GROUP], tsend.at[d % GROUP], trecv.at[d % GROUP], d)

    def tell(sem, d):
        pl.semaphore_signal(known.at[sem], inc=1, device_id=(block(d) * stride + rest,),
                            device_id_type=MESH)

    def for_slots(first, last, moves):
        def step(g, carry):
            for d in moves:
                slot_copy(d, g).start()
            return carry
        lax.fori_loop(first, last, step, 0)

    def wait_of(d):
        odd = rest // (stride // 2)
        wait = 0
        for parity, row in enumerate(LATER):
            for f, steps in enumerate(row):
                hit = jnp.logical_and(odd == parity, block(d) == f)
                wait = jnp.where(hit, steps, wait)
        return wait

    def in_order(moves):
        lags = [wait_of(d) for d, _ in moves]

        def step(k, carry):
            for (d, count), lag in zip(moves, lags):
                g = k - lag
                @pl.when(jnp.logical_and(g >= 0, g < count))
                def _(d=d, g=g):
                    slot_copy(d, g).start()
            return carry
        lax.fori_loop(0, GROUP + max(map(max, LATER)), step, 0)

    barrier = pltpu.get_barrier_semaphore()
    for d in (1, -1):
        pl.semaphore_signal(barrier, inc=1, device_id=(block(d) * stride + rest,),
                            device_id_type=MESH)
    boxes = [
        pltpu.make_async_copy(tbox_hbm, tbox, local.at[0]),
        pltpu.make_async_copy(sbox_hbm, sbox, local.at[1]),
    ]
    own_copy = pltpu.make_async_copy(
        coeffs.at[pl.ds(e_me * GROUP, GROUP)], got.at[0], local.at[2]
    )
    weights_copy = pltpu.make_async_copy(interp_hbm, interp, local.at[3])
    for copy in boxes:
        copy.start()
    own_copy.start()
    weights_copy.start()
    for copy in boxes:
        copy.wait()
    turn = (tbox[...] - sbox[...]) & 4095
    tab[0:1, :] = jnp.concatenate([turn[0:1], turn[1:2]], axis=1)
    tab[1:2, :] = jnp.concatenate([turn[2:3], turn[2:3]], axis=1)
    tabs[0] = tab[...]

    pl.semaphore_wait(barrier, 2)
    tell(0, 1)
    tell(1, -1)
    for d in (1, -1):
        table_copy(d).start()
    for_slots(4, 8, (1, -1))
    pl.semaphore_wait(known.at[0], 1)
    pl.semaphore_wait(known.at[1], 1)
    tell(2, 1)
    tell(3, -1)
    for d in (2, -2):
        table_copy(d).start()
    for_slots(6, 8, (2, -2))
    pl.semaphore_wait(known.at[2], 1)
    pl.semaphore_wait(known.at[3], 1)
    tell(4, 1)
    for d in (3, -3):
        table_copy(d).start()
    pl.semaphore_wait(known.at[4], 1)
    table_copy(4).start()
    in_order(((4, 8), (3, 8), (-3, 8), (2, 6), (-2, 6), (1, 4), (-1, 4)))

    weights_copy.wait()
    for l in range(3):
        for t in range(2):
            for c in range(2):
                wcat[l, c * 128:(c + 1) * 128, t * 128:(t + 1) * 128] = interp[l, t, c]

    for d in ALL:
        table_copy(d).wait_recv()
    angle = tabs[...].astype(jnp.float32) * (2.0 * math.pi / 4096.0)
    waves[0] = jnp.cos(angle)
    waves[1] = jnp.sin(angle)
    to_scalar = pltpu.make_async_copy(waves, phase, local.at[4])
    to_scalar.start()
    to_scalar.wait()
    own_copy.wait()

    sign = jnp.where(lax.broadcasted_iota(jnp.int32, (1, 128), 1) < 64, -1.0, 1.0)
    f0, f1, f2 = e_me // 4, e_me // 2 % 2, e_me % 2

    def turned(x, e, l, slot):
        at = (e_me - e + GROUP) % GROUP
        c = phase[0, at, l // 2, l % 2 * 64 + slot]
        s = phase[1, at, l // 2, l % 2 * 64 + slot]
        return (c * x + (s * sign) * pltpu.roll(x, 64, 1)).astype(jnp.bfloat16)

    def level(l, pieces):
        rows = jnp.concatenate([jnp.concatenate(p, axis=1) for p in pieces], axis=0)
        return jnp.dot(rows, wcat[l], preferred_element_type=jnp.float32)

    def work(g, carry):
        for d in ALL:
            slot_copy(d, g).wait_recv()
        y = level(0, [
            [turned(got[(e_me - e + GROUP) % GROUP, g].astype(jnp.float32), e, 0,
                    e_me * 8 + g)
             for e in (e1 * 2 + e2, 4 + e1 * 2 + e2)]
            for e1 in range(2) for e2 in range(2)
        ])
        y = level(1, [
            [turned(y[(e1 * 2 + e2) * 128:(e1 * 2 + e2 + 1) * 128, t0 * 128:(t0 + 1) * 128],
                    f0 * 4 + e1 * 2 + e2, 1, f1 * 32 + f2 * 16 + g * 2 + t0)
             for e1 in range(2)]
            for e2 in range(2) for t0 in range(2)
        ])
        y = level(2, [
            [turned(y[(e2 * 2 + t0) * 128:(e2 * 2 + t0 + 1) * 128, t1 * 128:(t1 + 1) * 128],
                    f0 * 4 + f1 * 2 + e2, 2, f2 * 32 + g * 4 + t0 * 2 + t1)
             for e2 in range(2)]
            for t0 in range(2) for t1 in range(2)
        ])
        for t01 in range(4):
            for t2 in range(2):
                out[g * 8 + t01 * 2 + t2] = y[
                    t01 * 128:(t01 + 1) * 128, t2 * 128:(t2 + 1) * 128
                ].astype(jnp.bfloat16)
        return carry

    lax.fori_loop(0, GROUP, work, 0)

    for d in ALL:
        table_copy(d).wait_send()

    def finish(g, carry):
        for d in ALL:
            slot_copy(d, g).wait_send()
        return carry

    lax.fori_loop(0, GROUP, finish, 0)


def solution(mesh):
    n = mesh.shape["pairs"]

    def body(coeffs, target_box, source_box, interp):
        _, rows, columns = coeffs.shape
        dma = pltpu.SemaphoreType.DMA
        return pl.pallas_call(
            functools.partial(kernel, n),
            out_shape=pltpu.VMEM(coeffs.shape, jnp.bfloat16),
            in_specs=[pl.BlockSpec(memory_space=pltpu.HBM)] * 4,
            out_specs=pl.BlockSpec(memory_space=pltpu.VMEM),
            scratch_shapes=[
                pltpu.VMEM(target_box.shape, jnp.int32),
                pltpu.VMEM(source_box.shape, jnp.int32),
                pltpu.VMEM(interp.shape, jnp.bfloat16),
                pltpu.VMEM((GROUP, GROUP, rows, columns), jnp.bfloat16),
                pltpu.VMEM((2, 128), jnp.int32),
                pltpu.VMEM((GROUP, 2, 128), jnp.int32),
                pltpu.VMEM((2, GROUP, 2, 128), jnp.float32),
                pltpu.SMEM((2, GROUP, 2, 128), jnp.float32),
                pltpu.VMEM((3, 256, 256), jnp.bfloat16),
                dma((GROUP, GROUP)),
                dma((GROUP, GROUP)),
                dma((GROUP,)),
                dma((GROUP,)),
                pltpu.SemaphoreType.REGULAR((5,)),
                dma((5,)),
            ],
            compiler_params=pltpu.CompilerParams(
                collective_id=0, has_side_effects=True, vmem_limit_bytes=32 << 20
            ),
            name="butterfly",
        )(*(
            pltpu.with_memory_space_constraint(a, pltpu.HBM)
            for a in (coeffs, target_box, source_box, interp)
        ))

    placed = (P("pairs", None, None), P(None, "pairs"), P(None, "pairs"), P())
    return jax.shard_map(
        body, mesh=mesh, in_specs=placed, out_specs=P("pairs", None, None), check_vma=False
    )
```

```python
import functools
import math

import jax
import jax.numpy as jnp
from jax import lax
from jax.experimental import pallas as pl
from jax.experimental.pallas import tpu as pltpu
from jax.sharding import PartitionSpec as P

MESH = pl.DeviceIdType.MESH
GROUP = 8
LATER = ((2, 6, 8, 10, 24, 22, 20, 20), (2, 5, 8, 10, 24, 28, 28, 20))
ALL = (1, -1, 2, -2, 3, -3, 4)


def kernel(n, coeffs, tbox_hbm, sbox_hbm, interp_hbm, out, tbox, sbox, interp, got, tab,
           tabs, waves, phase, wcat, send, recv, tsend, trecv, known, local):
    stride = n // GROUP
    me = lax.axis_index("pairs")
    e_me = me // stride
    rest = me % stride

    def block(d):
        return (e_me + d + GROUP) % GROUP

    def remote(src, dst, ssem, rsem, d):
        return pltpu.make_async_remote_copy(
            src_ref=src, dst_ref=dst, send_sem=ssem, recv_sem=rsem,
            device_id=(block(d) * stride + rest,), device_id_type=MESH,
        )

    def slot_copy(d, g):
        return remote(coeffs.at[block(d) * GROUP + g], got.at[d % GROUP, g],
                      send.at[d % GROUP, g], recv.at[d % GROUP, g], d)

    def table_copy(d):
        return remote(tab, tabs.at[d % GROUP], tsend.at[d % GROUP], trecv.at[d % GROUP], d)

    def tell(sem, d):
        pl.semaphore_signal(known.at[sem], inc=1, device_id=(block(d) * stride + rest,),
                            device_id_type=MESH)

    def for_slots(first, last, moves):
        def step(g, carry):
            for d in moves:
                slot_copy(d, g).start()
            return carry
        lax.fori_loop(first, last, step, 0)

    def wait_of(d):
        odd = rest // (stride // 2)
        wait = 0
        for parity, row in enumerate(LATER):
            for f, steps in enumerate(row):
                hit = jnp.logical_and(odd == parity, block(d) == f)
                wait = jnp.where(hit, steps, wait)
        return wait

    def in_order(moves):
        lags = [wait_of(d) for d, _ in moves]

        def step(k, carry):
            for (d, count), lag in zip(moves, lags):
                g = k - lag
                @pl.when(jnp.logical_and(g >= 0, g < count))
                def _(d=d, g=g):
                    slot_copy(d, g).start()
            return carry
        lax.fori_loop(0, GROUP + max(map(max, LATER)), step, 0)

    barrier = pltpu.get_barrier_semaphore()
    for d in (1, -1):
        pl.semaphore_signal(barrier, inc=1, device_id=(block(d) * stride + rest,),
                            device_id_type=MESH)
    boxes = [
        pltpu.make_async_copy(tbox_hbm, tbox, local.at[0]),
        pltpu.make_async_copy(sbox_hbm, sbox, local.at[1]),
    ]
    own_copy = pltpu.make_async_copy(
        coeffs.at[pl.ds(e_me * GROUP, GROUP)], got.at[0], local.at[2]
    )
    weights_copy = pltpu.make_async_copy(interp_hbm, interp, local.at[3])
    for copy in boxes:
        copy.start()
    own_copy.start()
    weights_copy.start()
    for copy in boxes:
        copy.wait()
    turn = (tbox[...] - sbox[...]) & 4095
    tab[0:1, :] = jnp.concatenate([turn[0:1], turn[1:2]], axis=1)
    tab[1:2, :] = jnp.concatenate([turn[2:3], turn[2:3]], axis=1)
    tabs[0] = tab[...]

    pl.semaphore_wait(barrier, 2)
    tell(0, 1)
    tell(1, -1)
    for d in (1, -1):
        table_copy(d).start()
    for_slots(4, 8, (1, -1))
    pl.semaphore_wait(known.at[0], 1)
    pl.semaphore_wait(known.at[1], 1)
    tell(2, 1)
    tell(3, -1)
    for d in (2, -2):
        table_copy(d).start()
    for_slots(6, 8, (2, -2))
    pl.semaphore_wait(known.at[2], 1)
    pl.semaphore_wait(known.at[3], 1)
    tell(4, 1)
    for d in (3, -3):
        table_copy(d).start()
    pl.semaphore_wait(known.at[4], 1)
    table_copy(4).start()
    in_order(((-3, 8), (3, 8), (-2, 6), (2, 6), (4, 8), (-1, 4), (1, 4)))

    weights_copy.wait()
    for l in range(3):
        for t in range(2):
            for c in range(2):
                wcat[l, c * 128:(c + 1) * 128, t * 128:(t + 1) * 128] = interp[l, t, c]

    for d in ALL:
        table_copy(d).wait_recv()
    angle = tabs[...].astype(jnp.float32) * (2.0 * math.pi / 4096.0)
    waves[0] = jnp.cos(angle)
    waves[1] = jnp.sin(angle)
    to_scalar = pltpu.make_async_copy(waves, phase, local.at[4])
    to_scalar.start()
    to_scalar.wait()
    own_copy.wait()

    sign = jnp.where(lax.broadcasted_iota(jnp.int32, (1, 128), 1) < 64, -1.0, 1.0)
    f0, f1, f2 = e_me // 4, e_me // 2 % 2, e_me % 2

    def turned(x, e, l, slot):
        at = (e_me - e + GROUP) % GROUP
        c = phase[0, at, l // 2, l % 2 * 64 + slot]
        s = phase[1, at, l // 2, l % 2 * 64 + slot]
        return (c * x + (s * sign) * pltpu.roll(x, 64, 1)).astype(jnp.bfloat16)

    def level(l, pieces):
        rows = jnp.concatenate([jnp.concatenate(p, axis=1) for p in pieces], axis=0)
        return jnp.dot(rows, wcat[l], preferred_element_type=jnp.float32)

    def work(g, carry):
        for d in ALL:
            slot_copy(d, g).wait_recv()
        y = level(0, [
            [turned(got[(e_me - e + GROUP) % GROUP, g].astype(jnp.float32), e, 0,
                    e_me * 8 + g)
             for e in (e1 * 2 + e2, 4 + e1 * 2 + e2)]
            for e1 in range(2) for e2 in range(2)
        ])
        y = level(1, [
            [turned(y[(e1 * 2 + e2) * 128:(e1 * 2 + e2 + 1) * 128, t0 * 128:(t0 + 1) * 128],
                    f0 * 4 + e1 * 2 + e2, 1, f1 * 32 + f2 * 16 + g * 2 + t0)
             for e1 in range(2)]
            for e2 in range(2) for t0 in range(2)
        ])
        y = level(2, [
            [turned(y[(e2 * 2 + t0) * 128:(e2 * 2 + t0 + 1) * 128, t1 * 128:(t1 + 1) * 128],
                    f0 * 4 + f1 * 2 + e2, 2, f2 * 32 + g * 4 + t0 * 2 + t1)
             for e2 in range(2)]
            for t0 in range(2) for t1 in range(2)
        ])
        for t01 in range(4):
            for t2 in range(2):
                out[g * 8 + t01 * 2 + t2] = y[
                    t01 * 128:(t01 + 1) * 128, t2 * 128:(t2 + 1) * 128
                ].astype(jnp.bfloat16)
        return carry

    lax.fori_loop(0, GROUP, work, 0)

    for d in ALL:
        table_copy(d).wait_send()

    def finish(g, carry):
        for d in ALL:
            slot_copy(d, g).wait_send()
        return carry

    lax.fori_loop(0, GROUP, finish, 0)


def solution(mesh):
    n = mesh.shape["pairs"]

    def body(coeffs, target_box, source_box, interp):
        _, rows, columns = coeffs.shape
        dma = pltpu.SemaphoreType.DMA
        return pl.pallas_call(
            functools.partial(kernel, n),
            out_shape=pltpu.VMEM(coeffs.shape, jnp.bfloat16),
            in_specs=[pl.BlockSpec(memory_space=pltpu.HBM)] * 4,
            out_specs=pl.BlockSpec(memory_space=pltpu.VMEM),
            scratch_shapes=[
                pltpu.VMEM(target_box.shape, jnp.int32),
                pltpu.VMEM(source_box.shape, jnp.int32),
                pltpu.VMEM(interp.shape, jnp.bfloat16),
                pltpu.VMEM((GROUP, GROUP, rows, columns), jnp.bfloat16),
                pltpu.VMEM((2, 128), jnp.int32),
                pltpu.VMEM((GROUP, 2, 128), jnp.int32),
                pltpu.VMEM((2, GROUP, 2, 128), jnp.float32),
                pltpu.SMEM((2, GROUP, 2, 128), jnp.float32),
                pltpu.VMEM((3, 256, 256), jnp.bfloat16),
                dma((GROUP, GROUP)),
                dma((GROUP, GROUP)),
                dma((GROUP,)),
                dma((GROUP,)),
                pltpu.SemaphoreType.REGULAR((5,)),
                dma((5,)),
            ],
            compiler_params=pltpu.CompilerParams(
                collective_id=0, has_side_effects=True, vmem_limit_bytes=32 << 20
            ),
            name="butterfly",
        )(*(
            pltpu.with_memory_space_constraint(a, pltpu.HBM)
            for a in (coeffs, target_box, source_box, interp)
        ))

    placed = (P("pairs", None, None), P(None, "pairs"), P(None, "pairs"), P())
    return jax.shard_map(
        body, mesh=mesh, in_specs=placed, out_specs=P("pairs", None, None), check_vma=False
    )
```
